32 devices in a mesh: grp: 2 (over x), reg: 4 (over y, core), sub: 4 (over z).
Axes of the slice: x: 2, y: 2, z: 4, core: 2. Of those that a mesh axis runs over, the one named last changes fastest.
Arguments:
- ensemble: float32 [128, 256, 512], P(('grp', 'reg'), None, 'sub'), parts along dimension 0, may hold values from -6 to 6
- stencil: float32 [9, 256], replicated, may hold values from -2 to 2
- forcing: float32 [256, 512], P(None, 'sub'), may hold values from -6 to 6
- obs_lat: int32 [1024], P('grp'), parts along dimension 0, may hold values from 0 to 255
- obs_lon: int32 [1024], P('grp'), parts along dimension 0, may hold values from 0 to 511
- obs_value: float32 [1024], P('grp'), parts along dimension 0, may hold values from -6 to 6
- obs_var: float32 [1024], P('grp'), parts along dimension 0, may hold values from 0.25 to 4
- obs_order: int32 [1024], P('grp'), parts along dimension 0, may hold values from 0 to 511, each once
Outputs:
- analysis: float32 [128, 256, 512], P('grp', 'reg', 'sub'), parts along dimension 0
The draws below stay inside these ranges and needn't reach their ends.
There are 2 independent parts, one for each index of `grp`. The reference program is written for one: setup_inputs(seed, part) draws one part's arguments, and reference() takes and returns one part's arrays. A program takes and returns all parts, laid end to end along the dimension named above; an argument that names none is the same for every part. Nothing has to cross between parts.
Inputs may be any that keep to these rules, and one draw needn't show every extreme that they name: `obs_order`: each of 0 to 511 appears once.
All inputs are finite; a program needn't handle non-finite values.
Results may differ from the reference program's by a relative error of at most 0.0003.
Values sent between devices are 32-bit elements; how exact they have to be, the bound alone decides.
A program may use at most 128 MiB of HBM per device.

```python
import math
import jax
import jax.numpy as jnp
from jax import lax

ENS = 64
LAT_DEV = 64
BATCH = 256
NBATCH = 2
NLAT = 256
NLON = 512
NOBS = 512
CLAT = 85
CLON = 64
N_REG = 4


def with_ends(entries, rng, low, largest):
    longest = entries.shape.index(max(entries.shape))
    spots = []
    for shift in (0, 1):
        where = [jax.random.randint(jax.random.fold_in(rng, axis), (), 0, length) for axis, length in enumerate(entries.shape)]
        where[longest] = (where[longest] + shift) % entries.shape[longest]
        spots.append(tuple(where))
    return entries.at[spots[0]].set(low).at[spots[1]].set(largest)


def shard_levels(key, shape, cuts, least, largest):
    factor_of = 1.0
    for dim, blocks in cuts:
        heights = jax.random.uniform(jax.random.fold_in(jax.random.fold_in(key, 6), dim), (blocks,), jnp.float32, least / len(cuts), largest / len(cuts))
        factor_of = factor_of * jnp.repeat(jnp.exp(heights), shape[dim] // blocks).reshape((-1,) + (1,) * (len(shape) - 1 - dim))
    return factor_of


def bell_draw(key, extent, width, bound, pieces=(), kind=jnp.bfloat16):
    result = width * jax.random.normal(key, extent, jnp.float32)
    if pieces:
        result = result * shard_levels(key, extent, pieces, -0.22, 0.18)
    return jnp.clip(result, -bound, bound).astype(kind)


def setup_inputs(seed: int = 0, part: int = 0) -> dict:
    key_list = jax.random.split(jax.random.key(seed), 9)
    part_splits = jax.random.split(jax.random.fold_in(key_list[8], part), 9)
    return {
        "ensemble": bell_draw(part_splits[0], (ENS, NLAT, NLON), 1.0, 6.0, ((0, 4), (2, 4)), jnp.float32),
        "stencil": bell_draw(key_list[1], (9, NLAT), 9 ** -0.5, 2.0, (), jnp.float32),
        "forcing": bell_draw(key_list[2], (NLAT, NLON), 1.0, 6.0, ((1, 4),), jnp.float32),
        "obs_lat": with_ends(jax.random.randint(part_splits[3], (NOBS,), 0, NLAT), jax.random.fold_in(part_splits[3], 1), 0, NLAT - 1).astype(jnp.int32),
        "obs_lon": with_ends(jax.random.randint(part_splits[4], (NOBS,), 0, NLON), jax.random.fold_in(part_splits[4], 1), 0, NLON - 1).astype(jnp.int32),
        "obs_value": bell_draw(part_splits[5], (NOBS,), 1.5, 6.0, (), jnp.float32),
        "obs_var": jnp.clip(jnp.exp(jax.random.uniform(part_splits[6], (NOBS,), jnp.float32, math.log(0.25), math.log(4.0))), 0.25, 4.0),
        "obs_order": jax.random.permutation(part_splits[7], NOBS).astype(jnp.int32),
    }


small_jitter = 1e-06

def gaspari_cohn(radius):
    square = radius * radius
    cube = square * radius
    fourth = cube * radius
    fifth = fourth * radius
    inner = -0.25 * fifth + 0.5 * fourth + 0.625 * cube - 5.0 / 3.0 * square + 1.0
    safe = jnp.maximum(radius, 1.0)
    outer = fifth / 12.0 - 0.5 * fourth + 0.625 * cube + 5.0 / 3.0 * square - 5.0 * radius + 4.0 - 2.0 / 3.0 / safe
    return jnp.where(radius <= 1.0, inner, jnp.where(radius < 2.0, outer, 0.0))

def localize(obs_rows, obs_cols, grid_rows, grid_cols, nlon, half_lat, half_lon):
    lat_gap = jnp.abs(obs_rows[:, None] - grid_rows[None, :]).astype(jnp.float32) / half_lat
    lon_apart = jnp.abs(obs_cols[:, None] - grid_cols[None, :])
    lon_gap = jnp.minimum(lon_apart, nlon - lon_apart).astype(jnp.float32) / half_lon
    radius = jnp.sqrt(lat_gap[:, :, None] * lat_gap[:, :, None] + lon_gap[:, None, :] * lon_gap[:, None, :])
    return gaspari_cohn(radius).reshape(obs_rows.shape[0], -1)

def obs_update(prior, values, variances, members):
    prior_mean = lax.optimization_barrier(jnp.mean(prior, axis=0))
    anomaly = prior - prior_mean
    spread = lax.optimization_barrier(jnp.sum(anomaly * anomaly, axis=0)) / (members - 1.0)
    combined = spread + variances
    post_mean = (prior_mean * variances + values * spread) / combined
    shrink = jnp.sqrt(variances / combined)
    shift_obs = post_mean - prior_mean + (shrink - 1.0) * anomaly
    return (anomaly, spread, shift_obs)

def regress(block, anomaly, spread, shift_obs, locality):
    members = block.shape[0]
    covar = jnp.dot(anomaly.T, block, precision=lax.Precision.HIGHEST, preferred_element_type=jnp.float32) / (members - 1.0)
    gain = covar * locality / (spread + small_jitter)[:, None]
    return block + jnp.dot(shift_obs, gain, precision=lax.Precision.HIGHEST, preferred_element_type=jnp.float32)

def learned_advance(padded, weights, forcing_part):
    rows_out = padded.shape[1] - 2
    cols_out = padded.shape[2] - 2
    tendency = forcing_part[None, :, :]
    for row_shift in range(3):
        for col_shift in range(3):
            tendency = tendency + weights[3 * row_shift + col_shift][None, :, None] * padded[:, row_shift:row_shift + rows_out, col_shift:col_shift + cols_out]
    return padded[:, 1:-1, 1:-1] + jnp.tanh(tendency)

def reference(ensemble, stencil, forcing, obs_lat, obs_lon, obs_value, obs_var, obs_order):
    members = ensemble.shape[0]
    padded = jnp.pad(ensemble, ((0, 0), (1, 1), (0, 0)))
    padded = jnp.concatenate([padded[:, :, -1:], padded, padded[:, :, :1]], axis=2)
    present_state = learned_advance(padded, stencil, forcing)
    grid_cols = jnp.arange(NLON, dtype=jnp.int32)
    for batch_index in range(NBATCH):
        chosen = obs_order[batch_index * BATCH:(batch_index + 1) * BATCH]
        obs_rows = obs_lat[chosen]
        obs_cols = obs_lon[chosen]
        cells = obs_rows * NLON + obs_cols
        prior = present_state.reshape(members, NLAT * NLON)[:, cells]
        anomaly, spread, shift_obs = obs_update(prior, obs_value[chosen], obs_var[chosen], members)
        bands = present_state.reshape(members, N_REG, LAT_DEV * NLON).transpose(1, 0, 2)

        def one_band(pair):
            block, band_index = pair
            grid_rows = band_index * LAT_DEV + jnp.arange(LAT_DEV, dtype=jnp.int32)
            locality = localize(obs_rows, obs_cols, grid_rows, grid_cols, NLON, CLAT, CLON)
            return regress(block, anomaly, spread, shift_obs, locality)
        updated = lax.map(one_band, (bands, jnp.arange(N_REG, dtype=jnp.int32)))
        present_state = updated.transpose(1, 0, 2).reshape(members, NLAT, NLON)
    return present_state
```

```python
import functools

import jax
import jax.numpy as jnp
from jax import lax
from jax.experimental import pallas as pl
from jax.experimental.pallas import tpu as pltpu
from jax.sharding import PartitionSpec as P

BATCH = 256
NBATCH = 2
CH = 8
LANES = 128
small_jitter = 1e-06
MESH = pl.DeviceIdType.MESH


def locality_of(u):
    u = jnp.minimum(u, 4.0)
    r = lax.rsqrt(jnp.maximum(u, 1e-12))
    q = u * r
    s = 0.5 * u - 5.0 / 3.0
    us = u * s
    inner = 1.0 + us + (u * q) * (0.625 - 0.25 * u)
    outer = 4.0 - us + q * (u * (0.625 + u * (1.0 / 12.0)) - 5.0) - (2.0 / 3.0) * r
    return jnp.where(u <= 1.0, inner, jnp.where(u < 4.0, outer, 0.0))


def split(value):
    hi = value.astype(jnp.bfloat16)
    lo = (value - hi.astype(jnp.float32)).astype(jnp.bfloat16)
    return hi, lo


def apply_update(x, lhs, shifts, locality):
    members = x.shape[0]
    hi, lo = split(x)
    rhs = jnp.concatenate([hi, lo, hi, lo], axis=0)
    gain = jnp.dot(lhs, rhs, preferred_element_type=jnp.float32) * locality
    g_hi, g_lo = split(gain)
    both = jnp.dot(shifts, g_hi, preferred_element_type=jnp.float32)
    rest = jnp.dot(shifts[:members], g_lo, preferred_element_type=jnp.float32)
    return x + both[:members] + both[members:] + rest


def kernel(
    dims, ens_ref, sten_ref, forc_ref, lat_ref, lon_ref, val_ref, var_ref, ord_ref, out_ref,
    ep, fc, xs, loc, wt, wb, hsend, hrecv, hp, edge_l, edge_r, obs, pall, p_sub, p_reg, lhs_s, shift_s, xw,
    ens_sem, h_ssem, h_rsem, b_ssem, b_rsem, ps_ssem, ps_rsem, pr_ssem, pr_rsem,
):
    reg_count, sub_count, mem, nlat, nlon, lat_dev, side, nobs = dims
    f32 = jnp.float32
    members = mem * reg_count
    nq = lat_dev // CH
    half = nq // 2
    me = lax.axis_index("reg")
    my_sub = lax.axis_index("sub")
    right = lax.rem(my_sub + 1, sub_count)
    left = lax.rem(my_sub + sub_count - 1, sub_count)

    load = pltpu.make_async_copy(ens_ref, ep.at[:, pl.ds(8, nlat), :], ens_sem)
    load.start()
    hrecv[...] = jnp.zeros_like(hrecv)

    barrier = pltpu.get_barrier_semaphore()
    for d in range(1, reg_count):
        pl.semaphore_signal(barrier, inc=1, device_id={"reg": lax.rem(me + d, reg_count)}, device_id_type=MESH)
    for d in range(1, sub_count):
        pl.semaphore_signal(barrier, inc=1, device_id={"sub": lax.rem(my_sub + d, sub_count)}, device_id_type=MESH)

    ep[:, 0:8, :] = jnp.zeros((mem, 8, LANES), f32)
    ep[:, nlat + 8 : nlat + 16, :] = jnp.zeros((mem, 8, LANES), f32)
    hp[0:8, :] = jnp.zeros((8, LANES), f32)
    hp[nlat + 8 : nlat + 16, :] = jnp.zeros((8, LANES), f32)
    lane = lax.broadcasted_iota(jnp.int32, (nlat, LANES), 1)
    load.wait()
    packed = jnp.zeros((nlat, LANES), f32)
    for m in range(mem):
        packed = jnp.where(lane == m, ep[m, 8 : nlat + 8, 0:1], packed)
        packed = jnp.where(lane == side + m, ep[m, 8 : nlat + 8, LANES - 1 : LANES], packed)
    hsend[...] = jnp.transpose(packed)[0 : 2 * side]
    pl.semaphore_wait(barrier, reg_count + sub_count - 2)

    to_left = pltpu.make_async_remote_copy(
        src_ref=hsend.at[pl.ds(0, side)], dst_ref=hrecv.at[pl.ds(side, side)],
        send_sem=h_ssem.at[0], recv_sem=h_rsem.at[1], device_id={"sub": left}, device_id_type=MESH)
    to_right = pltpu.make_async_remote_copy(
        src_ref=hsend.at[pl.ds(side, side)], dst_ref=hrecv.at[pl.ds(0, side)],
        send_sem=h_ssem.at[1], recv_sem=h_rsem.at[0], device_id={"sub": right}, device_id_type=MESH)
    to_left.start()
    to_right.start()

    obs[...] = jnp.zeros_like(obs)
    obs[0:1, :] = lat_ref[...].astype(f32)
    obs[1:2, :] = lon_ref[...].astype(f32)
    obs[2:3, :] = val_ref[...]
    obs[3:4, :] = var_ref[...]
    columns = jnp.transpose(obs[...])
    picked = lax.broadcasted_iota(jnp.int32, (nobs, nobs), 0) == ord_ref[...]
    for i in range(4):
        obs[i : i + 1, :] = jnp.sum(jnp.where(picked, columns[:, i : i + 1], 0.0), axis=0, keepdims=True)
    ordered = jnp.transpose(obs[...])
    lat_col = [ordered[b * BATCH : (b + 1) * BATCH, 0:1] for b in range(NBATCH)]
    lon_col = [ordered[b * BATCH : (b + 1) * BATCH, 1:2] for b in range(NBATCH)]
    scale_lat = 1.0 / (nlat // 3)
    scale_lon = 1.0 / (nlon // 8)
    lat_row = obs[0:1, :]
    lon_row = obs[1:2, :]

    wt[...] = jnp.zeros_like(wt)
    wt[0:9, :] = sten_ref[...]
    taps = jnp.transpose(wt[...])
    for t in range(9):
        wb[t] = jnp.broadcast_to(taps[:, t : t + 1], (nlat, LANES))

    to_left.wait()
    to_right.wait()
    hp[8 : nlat + 8, :] = jnp.transpose(hrecv[...])
    h_prev, h_cur, h_next = hp[7 : nlat + 7, :], hp[8 : nlat + 8, :], hp[9 : nlat + 9, :]
    edge_l[...] = wb[0] * h_prev + wb[3] * h_cur + wb[6] * h_next
    edge_r[...] = wb[2] * h_prev + wb[5] * h_cur + wb[8] * h_next

    small_lane = lax.broadcasted_iota(jnp.int32, (CH, LANES), 1)

    def forecast(q, d):
        target = lax.rem(me + d, reg_count)
        base = pl.multiple_of(target * lat_dev + q * CH, CH)
        rows = pl.ds(base, CH)
        block = ep[:, pl.ds(base, 3 * CH), :]
        before, now, after = block[:, CH - 1 : 2 * CH - 1], block[:, CH : 2 * CH], block[:, CH + 1 : 2 * CH + 1]

        def tapped(j):
            return wb[j, rows, :] * before + wb[3 + j, rows, :] * now + wb[6 + j, rows, :] * after

        from_left = pltpu.roll(tapped(0).reshape(mem * CH, LANES), 1, 1).reshape(mem, CH, LANES)
        from_right = pltpu.roll(tapped(2).reshape(mem * CH, LANES), LANES - 1, 1).reshape(mem, CH, LANES)
        middle = tapped(1) + forc_ref[rows, :]
        el, er = edge_l[rows, :], edge_r[rows, :]
        for m in range(mem):
            a = jnp.where(small_lane == 0, el[:, m : m + 1], from_left[m])
            b = jnp.where(small_lane == LANES - 1, er[:, side + m : side + m + 1], from_right[m])
            fc[m, rows, :] = now[m] + jnp.tanh(middle[m] + a + b)

    def band_copy(q, d):
        target = lax.rem(me + d, reg_count)
        base = pl.multiple_of(target * lat_dev + q * CH, CH)
        return pltpu.make_async_remote_copy(
            src_ref=fc.at[:, pl.ds(base, CH), :],
            dst_ref=xs.at[pl.ds(me * mem, mem), pl.ds(pl.multiple_of(q * CH, CH), CH), :],
            send_sem=b_ssem.at[q, target], recv_sem=b_rsem.at[q, me],
            device_id={"reg": target}, device_id_type=MESH)

    def band_arrival(q, d):
        source = lax.rem(me + d, reg_count)
        base = pl.multiple_of(source * lat_dev + q * CH, CH)
        return pltpu.make_async_remote_copy(
            src_ref=fc.at[:, pl.ds(base, CH), :],
            dst_ref=xs.at[pl.ds(source * mem, mem), pl.ds(pl.multiple_of(q * CH, CH), CH), :],
            send_sem=b_ssem.at[q, source], recv_sem=b_rsem.at[q, source],
            device_id={"reg": source}, device_id_type=MESH)

    @pl.loop(0, half)
    def _(q):
        @pl.loop(1, reg_count)
        def _(d):
            forecast(q, d)
            band_copy(q, d).start()

    @pl.loop(half, nq)
    def _(q):
        @pl.loop(1, reg_count)
        def _(d):
            forecast(q, d)

    @pl.loop(0, nq)
    def _(q):
        forecast(q, 0)

    first_col = (my_sub * LANES).astype(f32)
    here = (lax.broadcasted_iota(jnp.int32, (LANES, nobs), 0).astype(f32) + first_col) == lon_row
    here = jnp.where(here, 1.0, 0.0).astype(jnp.bfloat16)
    here = jnp.concatenate([here, here], axis=0)
    on_row = lax.broadcasted_iota(jnp.int32, (nlat, nobs), 0).astype(f32) == lat_row
    p_sub[0] = jnp.zeros_like(p_sub[0])

    @pl.loop(0, mem)
    def _(m):
        hi, lo = split(fc[m])
        found = jnp.dot(jnp.concatenate([hi, lo], axis=1), here, preferred_element_type=f32)
        p_sub[0, pl.ds(m, 1), :] = jnp.sum(jnp.where(on_row, found, 0.0), axis=0, keepdims=True)

    sub_copies = []
    for d in range(1, sub_count):
        sub_copies.append(pltpu.make_async_remote_copy(
            src_ref=p_sub.at[0], dst_ref=p_sub.at[d], send_sem=ps_ssem.at[d], recv_sem=ps_rsem.at[d],
            device_id={"sub": lax.rem(my_sub + d, sub_count)}, device_id_type=MESH))
        sub_copies[-1].start()

    own = pl.multiple_of(me * lat_dev, CH)
    xs[pl.ds(me * mem, mem), :, :] = fc[:, pl.ds(own, lat_dev), :]

    first_row = (me * lat_dev).astype(f32)
    lon_here = lax.broadcasted_iota(jnp.int32, (BATCH, LANES), 1).astype(f32) + first_col

    def lon_part(columns_a, columns_b):
        apart = jnp.abs(columns_a - columns_b)
        gap = jnp.minimum(apart, nlon - apart) * scale_lon
        return gap * gap

    def fill_locality(b, low, high):
        lon_sq = lon_part(lon_col[b], lon_here)
        lat_of = lat_col[b] - first_row

        @pl.loop(low, high)
        def _(r):
            gap = (lat_of - r.astype(f32)) * scale_lat
            loc[b, r] = locality_of(gap * gap + lon_sq)

    for copy in sub_copies:
        copy.wait()
    total = p_sub[0]
    for d in range(1, sub_count):
        total = total + p_sub[d]
    p_reg[me] = total
    reg_copies = []
    for d in range(1, reg_count):
        target = lax.rem(me + d, reg_count)
        reg_copies.append(pltpu.make_async_remote_copy(
            src_ref=p_reg.at[me], dst_ref=p_reg.at[me], send_sem=pr_ssem.at[target], recv_sem=pr_rsem.at[me],
            device_id={"reg": target}, device_id_type=MESH))
        reg_copies[-1].start()

    @pl.loop(half, nq)
    def _(q):
        @pl.loop(1, reg_count)
        def _(d):
            band_copy(q, d).start()

    for b in range(NBATCH):
        fill_locality(b, 0, lat_dev)

    for d in range(1, reg_count):
        source = lax.rem(me + d, reg_count)
        pltpu.make_async_remote_copy(
            src_ref=p_reg.at[source], dst_ref=p_reg.at[source], send_sem=pr_ssem.at[source],
            recv_sem=pr_rsem.at[source], device_id={"reg": source}, device_id_type=MESH).wait_recv()
    for j in range(reg_count):
        pall[j * mem : (j + 1) * mem, :] = p_reg[j, 0:mem, :]

    prior = pall[:, 0:BATCH]
    for b in range(NBATCH):
        here_b = slice(b * BATCH, (b + 1) * BATCH)
        values, variances = obs[2:3, here_b], obs[3:4, here_b]
        prior_mean = jnp.sum(prior, axis=0, keepdims=True) * (1.0 / members)
        anomaly = prior - prior_mean
        spread = jnp.sum(anomaly * anomaly, axis=0, keepdims=True) * (1.0 / (members - 1.0))
        combined = spread + variances
        post_mean = (prior_mean * variances + values * spread) / combined
        shift = post_mean - prior_mean + (jnp.sqrt(variances / combined) - 1.0) * anomaly
        scaled = anomaly / ((members - 1.0) * (spread + small_jitter))
        hi = scaled.astype(jnp.bfloat16).astype(f32)
        lo = scaled - hi
        lhs_s[b] = jnp.transpose(jnp.concatenate([hi, hi, lo, lo], axis=0)).astype(jnp.bfloat16)
        shift_s[b] = jnp.concatenate(split(shift), axis=0)
        if b + 1 < NBATCH:
            later = slice((b + 1) * BATCH, (b + 2) * BATCH)
            gap = (lat_col[b] - lat_row[:, later]) * scale_lat
            site = locality_of(gap * gap + lon_part(lon_col[b], lon_row[:, later]))
            prior = apply_update(pall[:, later], lhs_s[b], shift_s[b], site)

    @pl.loop(0, nq)
    def _(q):
        @pl.loop(1, reg_count)
        def _(d):
            band_arrival(q, d).wait_recv()

        rows = pl.ds(pl.multiple_of(q * CH, CH), CH)
        chunk = jnp.swapaxes(xs[:, rows, :], 0, 1)
        xw[...] = jnp.concatenate([chunk[i] for i in range(CH)], axis=1)

        @pl.loop(0, NBATCH)
        def _(b):
            locality = jnp.concatenate([loc[b, q * CH + i] for i in range(CH)], axis=1)
            xw[...] = apply_update(xw[...], lhs_s[b], shift_s[b], locality)

        x = xw[...]
        done = jnp.stack([x[:, i * LANES : (i + 1) * LANES] for i in range(CH)], axis=0)
        out_ref[:, rows, :] = jnp.swapaxes(done, 0, 1)

    for copy in reg_copies:
        copy.wait_send()

    @pl.loop(0, nq)
    def _(q):
        @pl.loop(1, reg_count)
        def _(d):
            band_copy(q, d).wait_send()


def per_device(reg_count, sub_count, ensemble, stencil, forcing, obs_lat, obs_lon, obs_value, obs_var, obs_order):
    mem, nlat, lon_dev = ensemble.shape
    nobs = obs_lat.shape[0]
    lat_dev = nlat // reg_count
    members = mem * reg_count
    side = -(-mem // 8) * 8
    nq = lat_dev // CH
    f32, bf16 = jnp.float32, jnp.bfloat16
    dims = (reg_count, sub_count, mem, nlat, lon_dev * sub_count, lat_dev, side, nobs)
    vmem = pl.BlockSpec(memory_space=pltpu.VMEM)
    dma = pltpu.SemaphoreType.DMA
    return pl.pallas_call(
        functools.partial(kernel, dims),
        out_shape=jax.ShapeDtypeStruct((members, lat_dev, lon_dev), f32),
        in_specs=[pl.BlockSpec(memory_space=pl.ANY)] + [vmem] * 7,
        out_specs=vmem,
        scratch_shapes=[
            pltpu.VMEM((mem, nlat + 16, LANES), f32),
            pltpu.VMEM((mem, nlat, LANES), f32),
            pltpu.VMEM((members, lat_dev, LANES), f32),
            pltpu.VMEM((NBATCH, lat_dev, BATCH, LANES), f32),
            pltpu.VMEM((LANES, nlat), f32),
            pltpu.VMEM((9, nlat, LANES), f32),
            pltpu.VMEM((2 * side, nlat), f32),
            pltpu.VMEM((LANES, nlat), f32),
            pltpu.VMEM((nlat + 16, LANES), f32),
            pltpu.VMEM((nlat, LANES), f32),
            pltpu.VMEM((nlat, LANES), f32),
            pltpu.VMEM((LANES, nobs), f32),
            pltpu.VMEM((members, nobs), f32),
            pltpu.VMEM((sub_count, side, nobs), f32),
            pltpu.VMEM((reg_count, side, nobs), f32),
            pltpu.VMEM((NBATCH, BATCH, 4 * members), bf16),
            pltpu.VMEM((NBATCH, 2 * members, BATCH), bf16),
            pltpu.VMEM((members, CH * LANES), f32),
            dma, dma((2,)), dma((2,)), dma((nq, reg_count)), dma((nq, reg_count)),
            dma((sub_count,)), dma((sub_count,)), dma((reg_count,)), dma((reg_count,)),
        ],
        compiler_params=pltpu.CompilerParams(
            collective_id=0, has_side_effects=True, vmem_limit_bytes=52 * 1024 * 1024
        ),
    )(
        ensemble, stencil, forcing, obs_lat.reshape(1, nobs), obs_lon.reshape(1, nobs),
        obs_value.reshape(1, nobs), obs_var.reshape(1, nobs), obs_order.reshape(1, nobs),
    )


def solution(mesh):
    return jax.shard_map(
        functools.partial(per_device, mesh.shape["reg"], mesh.shape["sub"]),
        mesh=mesh,
        in_specs=(
            P(("grp", "reg"), None, "sub"),
            P(),
            P(None, "sub"),
            P("grp"),
            P("grp"),
            P("grp"),
            P("grp"),
            P("grp"),
        ),
        out_specs=P("grp", "reg", "sub"),
        check_vma=False,
    )
```

```python
import functools

import jax
import jax.numpy as jnp
from jax import lax
from jax.experimental import pallas as pl
from jax.experimental.pallas import tpu as pltpu
from jax.sharding import PartitionSpec as P

BATCH = 256
NBATCH = 2
CH = 8
LANES = 128
small_jitter = 1e-06
MESH = pl.DeviceIdType.MESH


def locality_of(u):
    u = jnp.minimum(u, 4.0)
    r = lax.rsqrt(u)
    q = u * r
    s = 0.5 * u - 5.0 / 3.0
    us = u * s
    inner = 1.0 + us + (u * q) * (0.625 - 0.25 * u)
    outer = 4.0 - us + q * (u * (0.625 + u * (1.0 / 12.0)) - 5.0) - (2.0 / 3.0) * r
    return jnp.where(u <= 1.0, inner, outer)


def split(value):
    hi = value.astype(jnp.bfloat16)
    lo = (value - hi.astype(jnp.float32)).astype(jnp.bfloat16)
    return hi, lo


def apply_update(x, lhs, shifts, locality):
    members = x.shape[0]
    hi, lo = split(x)
    rhs = jnp.concatenate([hi, lo, hi, lo], axis=0)
    gain = jnp.dot(lhs, rhs, preferred_element_type=jnp.float32) * locality
    g_hi, g_lo = split(gain)
    both = jnp.dot(shifts, g_hi, preferred_element_type=jnp.float32)
    rest = jnp.dot(shifts[:members], g_lo, preferred_element_type=jnp.float32)
    return x + both[:members] + both[members:] + rest


def kernel(
    dims, ens_ref, sten_ref, forc_ref, lat_ref, lon_ref, val_ref, var_ref, ord_ref, out_ref,
    ep, fc, xs, loc, wt, wb, hsend, hrecv, hp, edge_l, edge_r, obs, pall, p_sub, p_reg, lhs_s, shift_s, xw,
    ens_sem, h_ssem, h_rsem, b_ssem, b_rsem, ps_ssem, ps_rsem, pr_ssem, pr_rsem,
):
    reg_count, sub_count, mem, nlat, nlon, lat_dev, side, nobs = dims
    f32 = jnp.float32
    members = mem * reg_count
    nq = lat_dev // CH
    half = nq // 2
    me = lax.axis_index("reg")
    my_sub = lax.axis_index("sub")
    right = lax.rem(my_sub + 1, sub_count)
    left = lax.rem(my_sub + sub_count - 1, sub_count)

    load = pltpu.make_async_copy(ens_ref, ep.at[:, pl.ds(8, nlat), :], ens_sem)
    load.start()
    hrecv[...] = jnp.zeros_like(hrecv)

    barrier = pltpu.get_barrier_semaphore()
    for d in range(1, reg_count):
        pl.semaphore_signal(barrier, inc=1, device_id={"reg": lax.rem(me + d, reg_count)}, device_id_type=MESH)
    for d in range(1, sub_count):
        pl.semaphore_signal(barrier, inc=1, device_id={"sub": lax.rem(my_sub + d, sub_count)}, device_id_type=MESH)

    ep[:, 0:8, :] = jnp.zeros((mem, 8, LANES), f32)
    ep[:, nlat + 8 : nlat + 16, :] = jnp.zeros((mem, 8, LANES), f32)
    hp[0:8, :] = jnp.zeros((8, LANES), f32)
    hp[nlat + 8 : nlat + 16, :] = jnp.zeros((8, LANES), f32)
    lane = lax.broadcasted_iota(jnp.int32, (nlat, LANES), 1)
    load.wait()
    packed = jnp.zeros((nlat, LANES), f32)
    for m in range(mem):
        packed = jnp.where(lane == m, ep[m, 8 : nlat + 8, 0:1], packed)
        packed = jnp.where(lane == side + m, ep[m, 8 : nlat + 8, LANES - 1 : LANES], packed)
    hsend[...] = jnp.transpose(packed)[0 : 2 * side]
    pl.semaphore_wait(barrier, reg_count + sub_count - 2)

    to_left = pltpu.make_async_remote_copy(
        src_ref=hsend.at[pl.ds(0, side)], dst_ref=hrecv.at[pl.ds(side, side)],
        send_sem=h_ssem.at[0], recv_sem=h_rsem.at[1], device_id={"sub": left}, device_id_type=MESH)
    to_right = pltpu.make_async_remote_copy(
        src_ref=hsend.at[pl.ds(side, side)], dst_ref=hrecv.at[pl.ds(0, side)],
        send_sem=h_ssem.at[1], recv_sem=h_rsem.at[0], device_id={"sub": right}, device_id_type=MESH)
    to_left.start()
    to_right.start()

    obs[...] = jnp.zeros_like(obs)
    obs[0:1, :] = lat_ref[...].astype(f32)
    obs[1:2, :] = lon_ref[...].astype(f32)
    obs[2:3, :] = val_ref[...]
    obs[3:4, :] = var_ref[...]
    columns = jnp.transpose(obs[...])
    picked = lax.broadcasted_iota(jnp.int32, (nobs, nobs), 0) == ord_ref[...]
    for i in range(4):
        obs[i : i + 1, :] = jnp.sum(jnp.where(picked, columns[:, i : i + 1], 0.0), axis=0, keepdims=True)
    ordered = jnp.transpose(obs[...])
    lat_col = [ordered[b * BATCH : (b + 1) * BATCH, 0:1] for b in range(NBATCH)]
    lon_col = [ordered[b * BATCH : (b + 1) * BATCH, 1:2] for b in range(NBATCH)]
    scale_lat = 1.0 / (nlat // 3)
    scale_lon = 1.0 / (nlon // 8)
    lat_row = obs[0:1, :]
    lon_row = obs[1:2, :]

    wt[...] = jnp.zeros_like(wt)
    wt[0:9, :] = sten_ref[...]
    taps = jnp.transpose(wt[...])
    for t in range(9):
        wb[t] = jnp.broadcast_to(taps[:, t : t + 1], (nlat, LANES))

    to_left.wait()
    to_right.wait()
    hp[8 : nlat + 8, :] = jnp.transpose(hrecv[...])
    h_prev, h_cur, h_next = hp[7 : nlat + 7, :], hp[8 : nlat + 8, :], hp[9 : nlat + 9, :]
    edge_l[...] = wb[0] * h_prev + wb[3] * h_cur + wb[6] * h_next
    edge_r[...] = wb[2] * h_prev + wb[5] * h_cur + wb[8] * h_next

    small_lane = lax.broadcasted_iota(jnp.int32, (CH, LANES), 1)

    def forecast(q, d):
        target = lax.rem(me + d, reg_count)
        base = pl.multiple_of(target * lat_dev + q * CH, CH)
        rows = pl.ds(base, CH)
        block = ep[:, pl.ds(base, 3 * CH), :]
        before, now, after = block[:, CH - 1 : 2 * CH - 1], block[:, CH : 2 * CH], block[:, CH + 1 : 2 * CH + 1]

        def tapped(j):
            return wb[j, rows, :] * before + wb[3 + j, rows, :] * now + wb[6 + j, rows, :] * after

        from_left = pltpu.roll(tapped(0).reshape(mem * CH, LANES), 1, 1).reshape(mem, CH, LANES)
        from_right = pltpu.roll(tapped(2).reshape(mem * CH, LANES), LANES - 1, 1).reshape(mem, CH, LANES)
        middle = tapped(1) + forc_ref[rows, :]
        el, er = edge_l[rows, :], edge_r[rows, :]
        for m in range(mem):
            a = jnp.where(small_lane == 0, el[:, m : m + 1], from_left[m])
            b = jnp.where(small_lane == LANES - 1, er[:, side + m : side + m + 1], from_right[m])
            fc[m, rows, :] = now[m] + jnp.tanh(middle[m] + a + b)

    def band_copy(q, d):
        target = lax.rem(me + d, reg_count)
        base = pl.multiple_of(target * lat_dev + q * CH, CH)
        return pltpu.make_async_remote_copy(
            src_ref=fc.at[:, pl.ds(base, CH), :],
            dst_ref=xs.at[pl.ds(me * mem, mem), pl.ds(pl.multiple_of(q * CH, CH), CH), :],
            send_sem=b_ssem.at[q, target], recv_sem=b_rsem.at[q, me],
            device_id={"reg": target}, device_id_type=MESH)

    def band_arrival(q, d):
        source = lax.rem(me + d, reg_count)
        base = pl.multiple_of(source * lat_dev + q * CH, CH)
        return pltpu.make_async_remote_copy(
            src_ref=fc.at[:, pl.ds(base, CH), :],
            dst_ref=xs.at[pl.ds(source * mem, mem), pl.ds(pl.multiple_of(q * CH, CH), CH), :],
            send_sem=b_ssem.at[q, source], recv_sem=b_rsem.at[q, source],
            device_id={"reg": source}, device_id_type=MESH)

    @pl.loop(0, half)
    def _(q):
        @pl.loop(1, reg_count)
        def _(d):
            forecast(q, d)
            band_copy(q, d).start()

    @pl.loop(half, nq)
    def _(q):
        @pl.loop(1, reg_count)
        def _(d):
            forecast(q, d)

    @pl.loop(0, nq)
    def _(q):
        forecast(q, 0)

    first_col = (my_sub * LANES).astype(f32)
    here = (lax.broadcasted_iota(jnp.int32, (LANES, nobs), 0).astype(f32) + first_col) == lon_row
    here = jnp.where(here, 1.0, 0.0).astype(jnp.bfloat16)
    here = jnp.concatenate([here, here], axis=0)
    on_row = lax.broadcasted_iota(jnp.int32, (nlat, nobs), 0).astype(f32) == lat_row
    p_sub[0] = jnp.zeros_like(p_sub[0])

    @pl.loop(0, mem)
    def _(m):
        hi, lo = split(fc[m])
        found = jnp.dot(jnp.concatenate([hi, lo], axis=1), here, preferred_element_type=f32)
        p_sub[0, pl.ds(m, 1), :] = jnp.sum(jnp.where(on_row, found, 0.0), axis=0, keepdims=True)

    sub_copies = []
    for d in range(1, sub_count):
        sub_copies.append(pltpu.make_async_remote_copy(
            src_ref=p_sub.at[0], dst_ref=p_sub.at[d], send_sem=ps_ssem.at[d], recv_sem=ps_rsem.at[d],
            device_id={"sub": lax.rem(my_sub + d, sub_count)}, device_id_type=MESH))
        sub_copies[-1].start()

    own = pl.multiple_of(me * lat_dev, CH)
    xs[pl.ds(me * mem, mem), :, :] = fc[:, pl.ds(own, lat_dev), :]

    first_row = (me * lat_dev).astype(f32)
    tiny = 1e-12
    lon_here = lax.broadcasted_iota(jnp.int32, (BATCH, LANES), 1).astype(f32) + first_col

    def lon_part(columns_a, columns_b):
        apart = jnp.abs(columns_a - columns_b)
        gap = jnp.minimum(apart, nlon - apart) * scale_lon
        return gap * gap + tiny

    def fill_locality(b, low, high):
        lon_sq = lon_part(lon_col[b], lon_here)
        lat_of = lat_col[b] - first_row

        @pl.loop(low, high)
        def _(r):
            gap = (lat_of - r.astype(f32)) * scale_lat
            loc[b, r] = locality_of(gap * gap + lon_sq)

    early = lat_dev // 2
    fill_locality(0, 0, early)
    for copy in sub_copies:
        copy.wait()
    total = p_sub[0]
    for d in range(1, sub_count):
        total = total + p_sub[d]
    p_reg[me] = total
    reg_copies = []
    for d in range(1, reg_count):
        target = lax.rem(me + d, reg_count)
        reg_copies.append(pltpu.make_async_remote_copy(
            src_ref=p_reg.at[me], dst_ref=p_reg.at[me], send_sem=pr_ssem.at[target], recv_sem=pr_rsem.at[me],
            device_id={"reg": target}, device_id_type=MESH))
        reg_copies[-1].start()

    @pl.loop(half, nq)
    def _(q):
        @pl.loop(1, reg_count)
        def _(d):
            band_copy(q, d).start()

    fill_locality(0, early, lat_dev)
    for b in range(1, NBATCH):
        fill_locality(b, 0, lat_dev)

    for d in range(1, reg_count):
        source = lax.rem(me + d, reg_count)
        pltpu.make_async_remote_copy(
            src_ref=p_reg.at[source], dst_ref=p_reg.at[source], send_sem=pr_ssem.at[source],
            recv_sem=pr_rsem.at[source], device_id={"reg": source}, device_id_type=MESH).wait_recv()
    for j in range(reg_count):
        pall[j * mem : (j + 1) * mem, :] = p_reg[j, 0:mem, :]

    prior = pall[:, 0:BATCH]
    for b in range(NBATCH):
        here_b = slice(b * BATCH, (b + 1) * BATCH)
        values, variances = obs[2:3, here_b], obs[3:4, here_b]
        prior_mean = jnp.sum(prior, axis=0, keepdims=True) * (1.0 / members)
        anomaly = prior - prior_mean
        spread = jnp.sum(anomaly * anomaly, axis=0, keepdims=True) * (1.0 / (members - 1.0))
        combined = spread + variances
        post_mean = (prior_mean * variances + values * spread) / combined
        shift = post_mean - prior_mean + (jnp.sqrt(variances / combined) - 1.0) * anomaly
        scaled = anomaly / ((members - 1.0) * (spread + small_jitter))
        hi = scaled.astype(jnp.bfloat16).astype(f32)
        lo = scaled - hi
        lhs_s[b] = jnp.transpose(jnp.concatenate([hi, hi, lo, lo], axis=0)).astype(jnp.bfloat16)
        shift_s[b] = jnp.concatenate(split(shift), axis=0)
        if b + 1 < NBATCH:
            later = slice((b + 1) * BATCH, (b + 2) * BATCH)
            gap = (lat_col[b] - lat_row[:, later]) * scale_lat
            site = locality_of(gap * gap + lon_part(lon_col[b], lon_row[:, later]))
            prior = apply_update(pall[:, later], lhs_s[b], shift_s[b], site)

    @pl.loop(0, nq)
    def _(q):
        @pl.loop(1, reg_count)
        def _(d):
            band_arrival(q, d).wait_recv()

        rows = pl.ds(pl.multiple_of(q * CH, CH), CH)
        chunk = jnp.swapaxes(xs[:, rows, :], 0, 1)
        xw[...] = jnp.concatenate([chunk[i] for i in range(CH)], axis=1)

        @pl.loop(0, NBATCH)
        def _(b):
            locality = jnp.concatenate([loc[b, q * CH + i] for i in range(CH)], axis=1)
            xw[...] = apply_update(xw[...], lhs_s[b], shift_s[b], locality)

        x = xw[...]
        done = jnp.stack([x[:, i * LANES : (i + 1) * LANES] for i in range(CH)], axis=0)
        out_ref[:, rows, :] = jnp.swapaxes(done, 0, 1)

    for copy in reg_copies:
        copy.wait_send()

    @pl.loop(0, nq)
    def _(q):
        @pl.loop(1, reg_count)
        def _(d):
            band_copy(q, d).wait_send()


def per_device(reg_count, sub_count, ensemble, stencil, forcing, obs_lat, obs_lon, obs_value, obs_var, obs_order):
    mem, nlat, lon_dev = ensemble.shape
    nobs = obs_lat.shape[0]
    lat_dev = nlat // reg_count
    members = mem * reg_count
    side = -(-mem // 8) * 8
    nq = lat_dev // CH
    f32, bf16 = jnp.float32, jnp.bfloat16
    dims = (reg_count, sub_count, mem, nlat, lon_dev * sub_count, lat_dev, side, nobs)
    vmem = pl.BlockSpec(memory_space=pltpu.VMEM)
    dma = pltpu.SemaphoreType.DMA
    return pl.pallas_call(
        functools.partial(kernel, dims),
        out_shape=jax.ShapeDtypeStruct((members, lat_dev, lon_dev), f32),
        in_specs=[pl.BlockSpec(memory_space=pltpu.HBM)] + [vmem] * 7,
        out_specs=vmem,
        scratch_shapes=[
            pltpu.VMEM((mem, nlat + 16, LANES), f32),
            pltpu.VMEM((mem, nlat, LANES), f32),
            pltpu.VMEM((members, lat_dev, LANES), f32),
            pltpu.VMEM((NBATCH, lat_dev, BATCH, LANES), f32),
            pltpu.VMEM((LANES, nlat), f32),
            pltpu.VMEM((9, nlat, LANES), f32),
            pltpu.VMEM((2 * side, nlat), f32),
            pltpu.VMEM((LANES, nlat), f32),
            pltpu.VMEM((nlat + 16, LANES), f32),
            pltpu.VMEM((nlat, LANES), f32),
            pltpu.VMEM((nlat, LANES), f32),
            pltpu.VMEM((LANES, nobs), f32),
            pltpu.VMEM((members, nobs), f32),
            pltpu.VMEM((sub_count, side, nobs), f32),
            pltpu.VMEM((reg_count, side, nobs), f32),
            pltpu.VMEM((NBATCH, BATCH, 4 * members), bf16),
            pltpu.VMEM((NBATCH, 2 * members, BATCH), bf16),
            pltpu.VMEM((members, CH * LANES), f32),
            dma, dma((2,)), dma((2,)), dma((nq, reg_count)), dma((nq, reg_count)),
            dma((sub_count,)), dma((sub_count,)), dma((reg_count,)), dma((reg_count,)),
        ],
        compiler_params=pltpu.CompilerParams(
            collective_id=0, has_side_effects=True, vmem_limit_bytes=52 * 1024 * 1024
        ),
    )(
        ensemble, stencil, forcing, obs_lat.reshape(1, nobs), obs_lon.reshape(1, nobs),
        obs_value.reshape(1, nobs), obs_var.reshape(1, nobs), obs_order.reshape(1, nobs),
    )


def solution(mesh):
    return jax.shard_map(
        functools.partial(per_device, mesh.shape["reg"], mesh.shape["sub"]),
        mesh=mesh,
        in_specs=(
            P(("grp", "reg"), None, "sub"),
            P(),
            P(None, "sub"),
            P("grp"),
            P("grp"),
            P("grp"),
            P("grp"),
            P("grp"),
        ),
        out_specs=P("grp", "reg", "sub"),
        check_vma=False,
    )
```

```python
import functools

import jax
import jax.numpy as jnp
from jax import lax
from jax.experimental import pallas as pl
from jax.experimental.pallas import tpu as pltpu
from jax.sharding import PartitionSpec as P

BATCH = 256
NBATCH = 2
CH = 8
LANES = 128
small_jitter = 1e-06
MESH = pl.DeviceIdType.MESH


def locality_of(u):
    u = jnp.minimum(u, 4.0)
    r = lax.rsqrt(u)
    q = u * r
    s = 0.5 * u - 5.0 / 3.0
    us = u * s
    near = u <= 1.0
    cubic = (u * q) * (0.625 + jnp.where(near, -0.25, 1.0 / 12.0) * u)
    return 1.0 + (cubic + jnp.where(near, us, 3.0 - us - 5.0 * q - (2.0 / 3.0) * r))

def split(value):
    hi = value.astype(jnp.bfloat16)
    lo = (value - hi.astype(jnp.float32)).astype(jnp.bfloat16)
    return hi, lo


def apply_update(x, lhs, shifts, locality):
    members = x.shape[0]
    hi, lo = split(x)
    rhs = jnp.concatenate([hi, lo, hi, lo], axis=0)
    gain = jnp.dot(lhs, rhs, preferred_element_type=jnp.float32) * locality
    g_hi, g_lo = split(gain)
    both = jnp.dot(shifts, g_hi, preferred_element_type=jnp.float32)
    rest = jnp.dot(shifts[:members], g_lo, preferred_element_type=jnp.float32)
    return x + both[:members] + both[members:] + rest


def kernel(
    dims, ens_ref, sten_ref, forc_ref, lat_ref, lon_ref, val_ref, var_ref, ord_ref, out_ref,
    ep, fc, xs, loc, wt, wb, hsend, hrecv, hp, edge_l, edge_r, obs, pall, p_sub, p_reg, lhs_s, shift_s, xw,
    ens_sem, h_ssem, h_rsem, b_ssem, b_rsem, ps_ssem, ps_rsem, pr_ssem, pr_rsem,
):
    reg_count, sub_count, mem, nlat, nlon, lat_dev, side, nobs = dims
    f32 = jnp.float32
    members = mem * reg_count
    nq = lat_dev // CH
    half = nq // 2
    me = lax.axis_index("reg")
    my_sub = lax.axis_index("sub")
    right = lax.rem(my_sub + 1, sub_count)
    left = lax.rem(my_sub + sub_count - 1, sub_count)

    load = pltpu.make_async_copy(ens_ref, ep.at[:, pl.ds(8, nlat), :], ens_sem)
    load.start()
    hrecv[...] = jnp.zeros_like(hrecv)

    barrier = pltpu.get_barrier_semaphore()
    for d in range(1, reg_count):
        pl.semaphore_signal(barrier, inc=1, device_id={"reg": lax.rem(me + d, reg_count)}, device_id_type=MESH)
    for d in range(1, sub_count):
        pl.semaphore_signal(barrier, inc=1, device_id={"sub": lax.rem(my_sub + d, sub_count)}, device_id_type=MESH)

    ep[:, 0:8, :] = jnp.zeros((mem, 8, LANES), f32)
    ep[:, nlat + 8 : nlat + 16, :] = jnp.zeros((mem, 8, LANES), f32)
    hp[0:8, :] = jnp.zeros((8, LANES), f32)
    hp[nlat + 8 : nlat + 16, :] = jnp.zeros((8, LANES), f32)
    lane = lax.broadcasted_iota(jnp.int32, (nlat, LANES), 1)
    load.wait()
    packed = jnp.zeros((nlat, LANES), f32)
    for m in range(mem):
        packed = jnp.where(lane == m, ep[m, 8 : nlat + 8, 0:1], packed)
        packed = jnp.where(lane == side + m, ep[m, 8 : nlat + 8, LANES - 1 : LANES], packed)
    hsend[...] = jnp.transpose(packed)[0 : 2 * side]
    pl.semaphore_wait(barrier, reg_count + sub_count - 2)

    to_left = pltpu.make_async_remote_copy(
        src_ref=hsend.at[pl.ds(0, side)], dst_ref=hrecv.at[pl.ds(side, side)],
        send_sem=h_ssem.at[0], recv_sem=h_rsem.at[1], device_id={"sub": left}, device_id_type=MESH)
    to_right = pltpu.make_async_remote_copy(
        src_ref=hsend.at[pl.ds(side, side)], dst_ref=hrecv.at[pl.ds(0, side)],
        send_sem=h_ssem.at[1], recv_sem=h_rsem.at[0], device_id={"sub": right}, device_id_type=MESH)
    to_left.start()
    to_right.start()

    obs[...] = jnp.zeros_like(obs)
    obs[0:1, :] = lat_ref[...].astype(f32)
    obs[1:2, :] = lon_ref[...].astype(f32)
    obs[2:3, :] = val_ref[...]
    obs[3:4, :] = var_ref[...]
    columns = jnp.transpose(obs[...])
    picked = lax.broadcasted_iota(jnp.int32, (nobs, nobs), 0) == ord_ref[...]
    for i in range(4):
        obs[i : i + 1, :] = jnp.sum(jnp.where(picked, columns[:, i : i + 1], 0.0), axis=0, keepdims=True)
    ordered = jnp.transpose(obs[...])
    lat_col = [ordered[b * BATCH : (b + 1) * BATCH, 0:1] for b in range(NBATCH)]
    lon_col = [ordered[b * BATCH : (b + 1) * BATCH, 1:2] for b in range(NBATCH)]
    scale_lat = 1.0 / (nlat // 3)
    scale_lon = 1.0 / (nlon // 8)
    lat_row = obs[0:1, :]
    lon_row = obs[1:2, :]

    wt[...] = jnp.zeros_like(wt)
    wt[0:9, :] = sten_ref[...]
    taps = jnp.transpose(wt[...])
    for t in range(9):
        wb[t] = jnp.broadcast_to(taps[:, t : t + 1], (nlat, LANES))

    to_left.wait()
    to_right.wait()
    hp[8 : nlat + 8, :] = jnp.transpose(hrecv[...])
    h_prev, h_cur, h_next = hp[7 : nlat + 7, :], hp[8 : nlat + 8, :], hp[9 : nlat + 9, :]
    edge_l[...] = wb[0] * h_prev + wb[3] * h_cur + wb[6] * h_next
    edge_r[...] = wb[2] * h_prev + wb[5] * h_cur + wb[8] * h_next

    small_lane = lax.broadcasted_iota(jnp.int32, (CH, LANES), 1)

    def forecast(q, d):
        target = lax.rem(me + d, reg_count)
        base = pl.multiple_of(target * lat_dev + q * CH, CH)
        rows = pl.ds(base, CH)
        block = ep[:, pl.ds(base, 3 * CH), :]
        before, now, after = block[:, CH - 1 : 2 * CH - 1], block[:, CH : 2 * CH], block[:, CH + 1 : 2 * CH + 1]

        def tapped(j):
            return wb[j, rows, :] * before + wb[3 + j, rows, :] * now + wb[6 + j, rows, :] * after

        from_left = pltpu.roll(tapped(0).reshape(mem * CH, LANES), 1, 1).reshape(mem, CH, LANES)
        from_right = pltpu.roll(tapped(2).reshape(mem * CH, LANES), LANES - 1, 1).reshape(mem, CH, LANES)
        middle = tapped(1) + forc_ref[rows, :]
        el, er = edge_l[rows, :], edge_r[rows, :]
        for m in range(mem):
            a = jnp.where(small_lane == 0, el[:, m : m + 1], from_left[m])
            b = jnp.where(small_lane == LANES - 1, er[:, side + m : side + m + 1], from_right[m])
            fc[m, rows, :] = now[m] + jnp.tanh(middle[m] + a + b)

    def band_copy(q, d):
        target = lax.rem(me + d, reg_count)
        base = pl.multiple_of(target * lat_dev + q * CH, CH)
        return pltpu.make_async_remote_copy(
            src_ref=fc.at[:, pl.ds(base, CH), :],
            dst_ref=xs.at[pl.ds(me * mem, mem), pl.ds(pl.multiple_of(q * CH, CH), CH), :],
            send_sem=b_ssem.at[q, target], recv_sem=b_rsem.at[q, me],
            device_id={"reg": target}, device_id_type=MESH)

    def band_arrival(q, d):
        source = lax.rem(me + d, reg_count)
        base = pl.multiple_of(source * lat_dev + q * CH, CH)
        return pltpu.make_async_remote_copy(
            src_ref=fc.at[:, pl.ds(base, CH), :],
            dst_ref=xs.at[pl.ds(source * mem, mem), pl.ds(pl.multiple_of(q * CH, CH), CH), :],
            send_sem=b_ssem.at[q, source], recv_sem=b_rsem.at[q, source],
            device_id={"reg": source}, device_id_type=MESH)

    @pl.loop(0, half)
    def _(q):
        @pl.loop(1, reg_count)
        def _(d):
            forecast(q, d)
            band_copy(q, d).start()

    @pl.loop(half, nq)
    def _(q):
        @pl.loop(1, reg_count)
        def _(d):
            forecast(q, d)

    @pl.loop(0, nq)
    def _(q):
        forecast(q, 0)

    first_col = (my_sub * LANES).astype(f32)
    here = (lax.broadcasted_iota(jnp.int32, (LANES, nobs), 0).astype(f32) + first_col) == lon_row
    here = jnp.where(here, 1.0, 0.0).astype(jnp.bfloat16)
    here = jnp.concatenate([here, here], axis=0)
    on_row = lax.broadcasted_iota(jnp.int32, (nlat, nobs), 0).astype(f32) == lat_row
    p_sub[0] = jnp.zeros_like(p_sub[0])

    @pl.loop(0, mem)
    def _(m):
        hi, lo = split(fc[m])
        found = jnp.dot(jnp.concatenate([hi, lo], axis=1), here, preferred_element_type=f32)
        p_sub[0, pl.ds(m, 1), :] = jnp.sum(jnp.where(on_row, found, 0.0), axis=0, keepdims=True)

    sub_copies = []
    for d in range(1, sub_count):
        sub_copies.append(pltpu.make_async_remote_copy(
            src_ref=p_sub.at[0], dst_ref=p_sub.at[d], send_sem=ps_ssem.at[d], recv_sem=ps_rsem.at[d],
            device_id={"sub": lax.rem(my_sub + d, sub_count)}, device_id_type=MESH))
        sub_copies[-1].start()

    own = pl.multiple_of(me * lat_dev, CH)
    xs[pl.ds(me * mem, mem), :, :] = fc[:, pl.ds(own, lat_dev), :]

    first_row = (me * lat_dev).astype(f32)
    tiny = 1e-12
    lon_here = lax.broadcasted_iota(jnp.int32, (BATCH, LANES), 1).astype(f32) + first_col

    def lon_part(columns_a, columns_b):
        apart = jnp.abs(columns_a - columns_b)
        gap = jnp.minimum(apart, nlon - apart) * scale_lon
        return gap * gap + tiny

    def fill_locality(b, low, high):
        lon_sq = lon_part(lon_col[b], lon_here)
        lat_of = (lat_col[b] - first_row) * scale_lat

        @pl.loop(low, high)
        def _(r):
            gap = lat_of - r.astype(f32) * scale_lat
            loc[b, r] = locality_of(gap * gap + lon_sq)

    early = lat_dev // 2
    fill_locality(0, 0, early)
    for copy in sub_copies:
        copy.wait()
    total = p_sub[0]
    for d in range(1, sub_count):
        total = total + p_sub[d]
    p_reg[me] = total
    reg_copies = []
    for d in range(1, reg_count):
        target = lax.rem(me + d, reg_count)
        reg_copies.append(pltpu.make_async_remote_copy(
            src_ref=p_reg.at[me], dst_ref=p_reg.at[me], send_sem=pr_ssem.at[target], recv_sem=pr_rsem.at[me],
            device_id={"reg": target}, device_id_type=MESH))
        reg_copies[-1].start()

    @pl.loop(half, nq)
    def _(q):
        @pl.loop(1, reg_count)
        def _(d):
            band_copy(q, d).start()

    fill_locality(0, early, lat_dev)
    for b in range(1, NBATCH):
        fill_locality(b, 0, lat_dev)

    for d in range(1, reg_count):
        source = lax.rem(me + d, reg_count)
        pltpu.make_async_remote_copy(
            src_ref=p_reg.at[source], dst_ref=p_reg.at[source], send_sem=pr_ssem.at[source],
            recv_sem=pr_rsem.at[source], device_id={"reg": source}, device_id_type=MESH).wait_recv()
    for j in range(reg_count):
        pall[j * mem : (j + 1) * mem, :] = p_reg[j, 0:mem, :]

    prior = pall[:, 0:BATCH]
    for b in range(NBATCH):
        here_b = slice(b * BATCH, (b + 1) * BATCH)
        values, variances = obs[2:3, here_b], obs[3:4, here_b]
        prior_mean = jnp.sum(prior, axis=0, keepdims=True) * (1.0 / members)
        anomaly = prior - prior_mean
        spread = jnp.sum(anomaly * anomaly, axis=0, keepdims=True) * (1.0 / (members - 1.0))
        combined = spread + variances
        post_mean = (prior_mean * variances + values * spread) / combined
        shift = post_mean - prior_mean + (jnp.sqrt(variances / combined) - 1.0) * anomaly
        scaled = anomaly / ((members - 1.0) * (spread + small_jitter))
        hi = scaled.astype(jnp.bfloat16).astype(f32)
        lo = scaled - hi
        lhs_s[b] = jnp.transpose(jnp.concatenate([hi, hi, lo, lo], axis=0)).astype(jnp.bfloat16)
        shift_s[b] = jnp.concatenate(split(shift), axis=0)
        if b + 1 < NBATCH:
            later = slice((b + 1) * BATCH, (b + 2) * BATCH)
            gap = (lat_col[b] - lat_row[:, later]) * scale_lat
            site = locality_of(gap * gap + lon_part(lon_col[b], lon_row[:, later]))
            prior = apply_update(pall[:, later], lhs_s[b], shift_s[b], site)

    @pl.loop(0, nq)
    def _(q):
        @pl.loop(1, reg_count)
        def _(d):
            band_arrival(q, d).wait_recv()

        rows = pl.ds(pl.multiple_of(q * CH, CH), CH)
        chunk = jnp.swapaxes(xs[:, rows, :], 0, 1)
        xw[...] = jnp.concatenate([chunk[i] for i in range(CH)], axis=1)

        @pl.loop(0, NBATCH)
        def _(b):
            locality = jnp.concatenate([loc[b, q * CH + i] for i in range(CH)], axis=1)
            xw[...] = apply_update(xw[...], lhs_s[b], shift_s[b], locality)

        x = xw[...]
        done = jnp.stack([x[:, i * LANES : (i + 1) * LANES] for i in range(CH)], axis=0)
        out_ref[:, rows, :] = jnp.swapaxes(done, 0, 1)

    for copy in reg_copies:
        copy.wait_send()

    @pl.loop(0, nq)
    def _(q):
        @pl.loop(1, reg_count)
        def _(d):
            band_copy(q, d).wait_send()


def per_device(reg_count, sub_count, ensemble, stencil, forcing, obs_lat, obs_lon, obs_value, obs_var, obs_order):
    mem, nlat, lon_dev = ensemble.shape
    nobs = obs_lat.shape[0]
    lat_dev = nlat // reg_count
    members = mem * reg_count
    side = -(-mem // 8) * 8
    nq = lat_dev // CH
    f32, bf16 = jnp.float32, jnp.bfloat16
    dims = (reg_count, sub_count, mem, nlat, lon_dev * sub_count, lat_dev, side, nobs)
    vmem = pl.BlockSpec(memory_space=pltpu.VMEM)
    dma = pltpu.SemaphoreType.DMA
    return pl.pallas_call(
        functools.partial(kernel, dims),
        out_shape=jax.ShapeDtypeStruct((members, lat_dev, lon_dev), f32),
        in_specs=[pl.BlockSpec(memory_space=pltpu.HBM)] + [vmem] * 7,
        out_specs=vmem,
        scratch_shapes=[
            pltpu.VMEM((mem, nlat + 16, LANES), f32),
            pltpu.VMEM((mem, nlat, LANES), f32),
            pltpu.VMEM((members, lat_dev, LANES), f32),
            pltpu.VMEM((NBATCH, lat_dev, BATCH, LANES), f32),
            pltpu.VMEM((LANES, nlat), f32),
            pltpu.VMEM((9, nlat, LANES), f32),
            pltpu.VMEM((2 * side, nlat), f32),
            pltpu.VMEM((LANES, nlat), f32),
            pltpu.VMEM((nlat + 16, LANES), f32),
            pltpu.VMEM((nlat, LANES), f32),
            pltpu.VMEM((nlat, LANES), f32),
            pltpu.VMEM((LANES, nobs), f32),
            pltpu.VMEM((members, nobs), f32),
            pltpu.VMEM((sub_count, side, nobs), f32),
            pltpu.VMEM((reg_count, side, nobs), f32),
            pltpu.VMEM((NBATCH, BATCH, 4 * members), bf16),
            pltpu.VMEM((NBATCH, 2 * members, BATCH), bf16),
            pltpu.VMEM((members, CH * LANES), f32),
            dma, dma((2,)), dma((2,)), dma((nq, reg_count)), dma((nq, reg_count)),
            dma((sub_count,)), dma((sub_count,)), dma((reg_count,)), dma((reg_count,)),
        ],
        compiler_params=pltpu.CompilerParams(
            collective_id=0, has_side_effects=True, vmem_limit_bytes=52 * 1024 * 1024
        ),
    )(
        ensemble, stencil, forcing, obs_lat.reshape(1, nobs), obs_lon.reshape(1, nobs),
        obs_value.reshape(1, nobs), obs_var.reshape(1, nobs), obs_order.reshape(1, nobs),
    )


def solution(mesh):
    return jax.shard_map(
        functools.partial(per_device, mesh.shape["reg"], mesh.shape["sub"]),
        mesh=mesh,
        in_specs=(
            P(("grp", "reg"), None, "sub"),
            P(),
            P(None, "sub"),
            P("grp"),
            P("grp"),
            P("grp"),
            P("grp"),
            P("grp"),
        ),
        out_specs=P("grp", "reg", "sub"),
        check_vma=False,
    )
```
